32 devices in a mesh: pairs: 8 (over y, x, core), band: 4 (over z).
Axes of the slice: x: 2, y: 2, z: 4, core: 2. Of those that a mesh axis runs over, the one named last changes fastest.
Arguments:
- spectra: bfloat16 [4096, 4, 1024], P('pairs', 'band'), may hold values from -15 to 15
- observed: bfloat16 [16384, 4, 1024], P('pairs', 'band'), may hold values from -5 to 5
- pair_owner: int32 [16384, 2], P('pairs'), may hold values from 0 to 7, all different within a row; in each aligned block of 2048 rows (0 to 2047, 2048 to 4095, ...) at most 768 rows name the same one
- pair_slot: int32 [16384, 2], P('pairs'), may hold values from 0 to 511
- win_start: int32 [16384], P('pairs'), may hold values from 0 to 511
- win_end: int32 [16384], P('pairs'), may hold values from 513 to 1024
Outputs:
- noise_kernel: float32 [4096, 4, 512], P('pairs', 'band')
The draws below stay inside these ranges and needn't reach their ends.
Inputs may be any that keep to these rules, and one draw needn't show every extreme that they name: `pair_owner`: the two stations of a pair have different owners; among the pairs of one index of pairs no owner is named more than 768 times, a bound that some block reaches.
All inputs are finite; a program needn't handle non-finite values.
Results may differ from the reference program's by a relative error of at most 0.006.
Values may be sent and summed in bfloat16 or wider, within the bound.
A program may use at most 128 MiB of HBM per device.

```python
import math
import jax
import jax.numpy as jnp
import numpy as np
from jax import lax

F = 512
LAGS = 1024
STA_DEV = 512
P_DEV = 2048
CAP = 768
STATIONS = 4096
BANDS = 4
PAIRS = 16384
N_PAIRS = 8


def draw_spectra(key, part):
    key_base, key_scale = jax.random.split(jax.random.fold_in(key, 17))
    base = jnp.clip(jax.random.normal(key_base, (STATIONS, BANDS, 2 * F), jnp.float32), -5.0, 5.0)
    station_scale = jnp.exp(jax.random.uniform(key_scale, (STATIONS, 1, 1), jnp.float32, math.log(0.3), math.log(3.0)))
    falloff = jnp.exp(-math.log(3.0) * jnp.arange(BANDS, dtype=jnp.float32) / max(BANDS - 1, 1))[None, :, None]
    return (base * station_scale * falloff).astype(jnp.bfloat16)


def touch_ends(drawn, rng, least, high):
    longest = drawn.shape.index(max(drawn.shape))
    spots = []
    for shift in (0, 1):
        where = [jax.random.randint(jax.random.fold_in(rng, axis), (), 0, length) for axis, length in enumerate(drawn.shape)]
        where[longest] = (where[longest] + shift) % drawn.shape[longest]
        spots.append(tuple(where))
    return drawn.at[spots[0]].set(least).at[spots[1]].set(high)


def levels(own_key, shape, cuts, least, high):
    gain, own = 1.0, jax.random.fold_in(own_key, 6)
    for axis_at, blocks in cuts:
        draws = jnp.exp(jax.random.uniform(jax.random.fold_in(own, axis_at), (blocks,), jnp.float32, least / len(cuts), high / len(cuts)))
        gain = gain * jnp.repeat(draws, shape[axis_at] // blocks).reshape([-1 if axis == axis_at else 1 for axis in range(len(shape))])
    return gain


def deal_out(rng, own, number, rows, number_of, top, limit, skew):
    order = jax.random.permutation(rng, number_of)
    packed, common = shares(number_of, rows * top, limit, skew, True), shares(number_of, rows * top, limit, skew, False)
    places = jnp.arange(number_of)

    def named(sizes, offset_by):
        used = int((sizes > 0).sum())
        fixed = max(1, used // 4)
        shifted = fixed + (places - fixed + offset_by * (used - fixed)) % max(1, number_of - fixed)
        return jnp.zeros((number_of,), jnp.int32).at[order[jnp.where(places < fixed, places, shifted)]].set(jnp.asarray(sizes, jnp.int32))

    sizes = jnp.where(number % 4 == 0, named(packed, number // 4), named(common, number - number // 4 - 1))
    mixed = jax.random.permutation(jax.random.fold_in(own, 3), number_of)
    source_of, taker = mixed[0:number_of // 2 * 2:2], mixed[1:number_of // 2 * 2:2]
    room = jnp.minimum(sizes[source_of] - 1, limit - sizes[taker]) // 2
    room = jnp.where((source_of == order[0]) | (taker == order[0]) | (sizes[taker] == 0), 0, jnp.maximum(room, 0))
    shifted = jax.random.randint(jax.random.fold_in(own, 4), (number_of // 2,), 0, 1 << 20) % (room + 1)
    sizes = sizes.at[source_of].add(-shifted).at[taker].add(shifted)
    members = jnp.searchsorted(jnp.cumsum(sizes), jnp.arange(rows * top), side="right").astype(jnp.int32)
    grid = members.reshape(top, rows).T
    grid = grid[jax.random.permutation(jax.random.fold_in(own, 1), rows)]
    offset_by = jax.random.randint(jax.random.fold_in(own, 2), (rows, 1), 0, top)
    return jnp.take_along_axis(grid, (jnp.arange(top)[None, :] + offset_by) % top, axis=1)


def shares(amount, total, bound, lean, full):
    portions = [(1 << 20) // math.isqrt(grade ** lean) + 1 for grade in range(1, amount + 1)]
    largest = bound if full else min(bound, max(-(-total // amount), total * portions[0] // sum(portions)))
    least = 1 if total - largest >= amount - 1 else 0
    counts, surplus = [largest] + [least] * (amount - 1), total - largest - least * (amount - 1)
    while surplus > 0:
        candidates = [i for i in range(1, amount) if counts[i] < largest] or [i for i in range(1, amount) if counts[i] < bound]
        whole, left = sum([portions[i] for i in candidates]), surplus
        for i in candidates:
            more = min(bound - counts[i], max(1, left * portions[i] // whole), surplus)
            counts[i] = counts[i] + more
            surplus = surplus - more
    return np.array(counts)


def normal_values(own_key, shape, scale, most, cuts=(), kind=jnp.bfloat16):
    drawn = scale * jax.random.normal(own_key, shape, jnp.float32)
    if cuts:
        drawn = drawn * levels(own_key, shape, cuts, -0.22, 0.18)
    return jnp.clip(drawn, -most, most).astype(kind)


def setup_inputs(seed: int = 0) -> dict:
    streams_of = jax.random.split(jax.random.key(seed), 7)
    spectra = draw_spectra(jax.random.fold_in(streams_of[6], 71), 0)
    observed = normal_values(streams_of[1], (PAIRS, BANDS, LAGS), 0.7, 5.0, ((0, 8), (1, 4)))
    pair_owner_keys = jax.random.split(jax.random.fold_in(streams_of[2], 1), PAIRS // P_DEV)
    pair_owner_turns = jax.random.permutation(jax.random.fold_in(streams_of[2], 3), PAIRS // P_DEV)
    pair_owner = jax.vmap(lambda own, number: deal_out(jax.random.fold_in(streams_of[2], 2), own, number, P_DEV, N_PAIRS, 2, CAP, 2))(pair_owner_keys, pair_owner_turns).reshape((PAIRS, 2))
    pair_slot = touch_ends(jax.random.randint(streams_of[3], (PAIRS, 2), 0, STA_DEV), jax.random.fold_in(streams_of[3], 1), 0, STA_DEV - 1).astype(jnp.int32)
    win_start = touch_ends(jax.random.randint(streams_of[4], (PAIRS,), 0, LAGS // 2), jax.random.fold_in(streams_of[4], 1), 0, (LAGS // 2) - 1).astype(jnp.int32)
    win_end = touch_ends(jax.random.randint(streams_of[5], (PAIRS,), LAGS // 2 + 1, LAGS + 1), jax.random.fold_in(streams_of[5], 1), LAGS // 2 + 1, LAGS).astype(jnp.int32)
    return {"spectra": spectra, "observed": observed, "pair_owner": pair_owner, "pair_slot": pair_slot, "win_start": win_start, "win_end": win_end}


def lag_basis(half_width, lag_count):
    freqs = jnp.arange(half_width, dtype=jnp.int32)
    lag_index = jnp.arange(lag_count, dtype=jnp.int32)
    phases = (freqs[:, None] * lag_index[None, :] % lag_count).astype(jnp.float32) * (2.0 * math.pi / lag_count)
    factor = 1.0 / math.sqrt(lag_count)
    return jnp.concatenate([jnp.cos(phases) * factor, -jnp.sin(phases) * factor], axis=0).astype(jnp.bfloat16)

def reference(spectra, observed, pair_owner, pair_slot, win_start, win_end):
    spectrum = spectra.astype(jnp.float32)
    powers = lax.optimization_barrier(jnp.sum(spectrum * spectrum, axis=(1, 2))) / (BANDS * 2 * F)
    whitened = (spectrum * lax.rsqrt(powers + 1e-05)[:, None, None]).astype(jnp.bfloat16)
    endpoints = (pair_owner * STA_DEV + pair_slot).astype(jnp.int32)
    table = lag_basis(F, LAGS)
    lag_index = jnp.arange(LAGS, dtype=jnp.int32)
    window = ((lag_index[None, :] >= win_start[:, None]) & (lag_index[None, :] < win_end[:, None])).astype(jnp.float32)
    slot_ids = jnp.concatenate([endpoints[:, 0], endpoints[:, 1]])

    def one_band(band_index):
        band_spec = whitened[:, band_index, :]
        near_end = band_spec[endpoints[:, 0]].astype(jnp.float32)
        far_end = band_spec[endpoints[:, 1]].astype(jnp.float32)
        near_re, near_im = (near_end[:, :F], near_end[:, F:])
        far_re, far_im = (far_end[:, :F], far_end[:, F:])
        cross_spec = jnp.concatenate([near_re * far_re + near_im * far_im, near_im * far_re - near_re * far_im], axis=1).astype(jnp.bfloat16)
        lagged = jnp.dot(cross_spec, table, preferred_element_type=jnp.float32)
        observed_band = observed[:, band_index, :].astype(jnp.float32)
        residual = (window * (lagged - observed_band)).astype(jnp.bfloat16)
        adjoint = jnp.dot(residual, table.T, preferred_element_type=jnp.float32)
        adj_re, adj_im = (adjoint[:, :F], adjoint[:, F:])
        to_first = jnp.concatenate([adj_re * far_re - adj_im * far_im, adj_re * far_im + adj_im * far_re], axis=1).astype(jnp.bfloat16)
        to_second = jnp.concatenate([adj_re * near_re + adj_im * near_im, adj_re * near_im - adj_im * near_re], axis=1).astype(jnp.bfloat16)
        contribs = jnp.concatenate([to_first, to_second], axis=0).astype(jnp.float32)
        summed = jax.ops.segment_sum(contribs, slot_ids, num_segments=STATIONS)
        own_spec = band_spec.astype(jnp.float32)
        return 0.25 * (summed[:, :F] * own_spec[:, :F] + summed[:, F:] * own_spec[:, F:])
    kernels = lax.map(one_band, jnp.arange(BANDS, dtype=jnp.int32))
    return jnp.transpose(kernels, (1, 0, 2))
```

```python
import functools
import math

import jax
import jax.numpy as jnp
import numpy as np
from jax import lax
from jax.experimental import pallas as pl
from jax.experimental.pallas import tpu as pltpu
from jax.sharding import PartitionSpec as P

MESH = pl.DeviceIdType.MESH
VMEM_LIMIT = 60 * 1024 * 1024


def basis_constant(half_width, lag_count):
    phases = (np.arange(half_width)[:, None] * np.arange(lag_count)[None, :] % lag_count) * (
        2.0 * math.pi / lag_count
    )
    factor = 1.0 / math.sqrt(lag_count)
    table = np.concatenate([np.cos(phases) * factor, -np.sin(phases) * factor], axis=0)
    return table.astype(np.float32)


def neighbours(me):
    core, x, y = me % 2, (me // 2) % 2, me // 4
    across, along = me + 2 - 4 * x, me + 4 - 8 * y
    return across, along, across + 4 - 8 * y, me + 1 - 2 * core


def gather_kernel(
    bands, entries, owners, spec_ref, src_ref, arr_ref, scale_ref,
    part, part_recv, total, total_recv,
    local_sem, send_sem, recv_sem, band_send, band_recv, total_send, total_recv_sem,
):
    me = lax.axis_index("pairs")
    band = lax.axis_index("band")
    across, along, diagonal, sibling = neighbours(me)
    half = src_ref.shape[0] // 2

    barrier = pltpu.get_barrier_semaphore()
    for k in range(1, owners):
        pl.semaphore_signal(
            barrier, inc=1, device_id={"pairs": lax.rem(me + k, owners)}, device_id_type=MESH
        )
    for k in range(1, bands):
        pl.semaphore_signal(
            barrier, inc=1, device_id={"band": lax.rem(band + k, bands)}, device_id_type=MESH
        )
    pl.semaphore_wait(barrier, owners + bands - 2)

    def rows(part_index):
        return pl.ds(part_index * half, half)

    def push(src, owner, part_index, sem, target):
        copy = pltpu.make_async_remote_copy(
            src_ref=src,
            dst_ref=arr_ref.at[owner, rows(part_index)],
            send_sem=send_sem.at[sem[0]],
            recv_sem=recv_sem.at[sem[1]],
            device_id={"pairs": target},
            device_id_type=MESH,
        )
        copy.start()
        return copy

    def arrived(owner, part_index, sem):
        slot = arr_ref.at[owner, rows(part_index)]
        pltpu.make_async_remote_copy(
            src_ref=slot, dst_ref=slot, send_sem=send_sem.at[0], recv_sem=recv_sem.at[sem],
            device_id={"pairs": me + 1 - 2 * (me % 2)}, device_id_type=MESH,
        ).wait_recv()

    sent = []
    own = [src_ref.at[rows(0)], src_ref.at[rows(1)]]
    sent.append(push(own[0], me, 0, (0, 0), across))
    sent.append(push(own[1], me, 1, (1, 3), along))
    sent.append(push(own[1], me, 1, (2, 1), across))
    sent.append(push(own[0], me, 0, (3, 2), along))
    sent.append(push(own[0], me, 0, (4, 6), sibling))
    sent.append(push(own[1], me, 1, (5, 7), sibling))
    local = pltpu.make_async_copy(src_ref, arr_ref.at[me], local_sem)
    local.start()

    spectrum = spec_ref[...].astype(jnp.float32)
    square = spectrum * spectrum
    high = square.astype(jnp.bfloat16)
    low = (square - high.astype(jnp.float32)).astype(jnp.bfloat16)
    ones = jnp.ones((8, spec_ref.shape[1]), jnp.bfloat16)
    dims = (((1,), (1,)), ((), ()))
    part[...] = lax.dot_general(
        ones, high, dims, preferred_element_type=jnp.float32
    ) + lax.dot_general(ones, low, dims, preferred_element_type=jnp.float32)
    copies = []
    for k in range(1, bands):
        copy = pltpu.make_async_remote_copy(
            src_ref=part, dst_ref=part_recv.at[k], send_sem=band_send.at[k],
            recv_sem=band_recv.at[k],
            device_id={"band": lax.rem(band + k, bands)}, device_id_type=MESH,
        )
        copy.start()
        copies.append(copy)
    for copy in copies:
        copy.wait()
    power = part[...]
    for k in range(1, bands):
        power = power + part_recv[k]
    total[...] = lax.rsqrt(power / entries + 1e-05)
    copies = []
    for k in range(1, owners):
        copy = pltpu.make_async_remote_copy(
            src_ref=total, dst_ref=total_recv.at[me], send_sem=total_send.at[k],
            recv_sem=total_recv_sem.at[k],
            device_id={"pairs": lax.rem(me + k, owners)}, device_id_type=MESH,
        )
        copy.start()
        copies.append(copy)

    arrived(across, 0, 0)
    sent.append(push(arr_ref.at[across, rows(0)], across, 0, (6, 4), along))
    sent.append(push(arr_ref.at[across, rows(0)], across, 0, (7, 8), sibling))
    arrived(along, 1, 3)
    sent.append(push(arr_ref.at[along, rows(1)], along, 1, (8, 5), across))
    sent.append(push(arr_ref.at[along, rows(1)], along, 1, (9, 11), sibling))
    arrived(across, 1, 1)
    sent.append(push(arr_ref.at[across, rows(1)], across, 1, (10, 9), sibling))
    arrived(along, 0, 2)
    sent.append(push(arr_ref.at[along, rows(0)], along, 0, (11, 10), sibling))
    for k in range(1, owners):
        copies[k - 1].wait()
    for o in range(owners):
        scale_ref[o] = jnp.where(me == o, total[...], total_recv[o])
    arrived(diagonal, 0, 4)
    sent.append(push(arr_ref.at[diagonal, rows(0)], diagonal, 0, (12, 12), sibling))
    arrived(diagonal, 1, 5)
    sent.append(push(arr_ref.at[diagonal, rows(1)], diagonal, 1, (13, 13), sibling))
    shift = 1 - 2 * (me % 2)
    for index, chip in enumerate((me, across, along, diagonal)):
        arrived(chip + shift, 0, 6 + 2 * index)
        arrived(chip + shift, 1, 7 + 2 * index)
    for copy in sent:
        copy.wait_send()
    local.wait()


def pair_kernel(
    ids_ref, arr_ref, scale_ref, observed_ref, window_ref, table_ref, back_ref, out_ref,
    panel, near, far, cross,
):
    step = pl.program_id(0)
    owners, stations, width = arr_ref.shape
    tile = observed_ref.shape[0]
    groups = width // 128
    fold = groups // 2
    half = width // 2
    chunk = 64

    @pl.when(step == 0)
    def _():
        def whiten(o, carry):
            scale = scale_ref[o].T[:, 0:1]
            for r in range(0, stations, chunk):
                rows = arr_ref[o, r : r + chunk, :].astype(jnp.float32) * scale[r : r + chunk]
                rows = rows.astype(jnp.bfloat16).astype(jnp.float32)
                for j in range(groups):
                    first = (o * stations + r) * groups + j
                    panel[pl.ds(first, chunk, stride=groups), :] = rows[:, j * 128 : j * 128 + 128]
            return carry

        lax.fori_loop(0, owners, whiten, 0)

    pairs = ids_ref.shape[0] // 2

    def fetch(i, carry):
        for u in range(16):
            p = i * 16 + u
            here = pl.ds(pl.multiple_of(p * groups, groups), groups)
            a = pl.multiple_of(ids_ref[step * tile + p], groups)
            b = pl.multiple_of(ids_ref[pairs + step * tile + p], groups)
            near[here, :] = panel[pl.ds(a, groups), :]
            far[here, :] = panel[pl.ds(b, groups), :]
        return carry

    lax.fori_loop(0, tile // 16, fetch, 0)

    def multiply(i, carry):
        rows = pl.ds(pl.multiple_of(i * chunk, chunk), chunk)
        for j in range(fold):
            re = pl.ds(i * chunk * groups + j, chunk, stride=groups)
            im = pl.ds(i * chunk * groups + j + fold, chunk, stride=groups)
            ar, ai, br, bi = near[re, :], near[im, :], far[re, :], far[im, :]
            cross[rows, j * 128 : j * 128 + 128] = (ar * br + ai * bi).astype(jnp.bfloat16)
            cross[rows, half + j * 128 : half + j * 128 + 128] = (ai * br - ar * bi).astype(
                jnp.bfloat16
            )
        return carry

    lax.fori_loop(0, tile // chunk, multiply, 0)

    lagged = jnp.dot(cross[...], table_ref[...], preferred_element_type=jnp.float32)
    lag = lax.broadcasted_iota(jnp.int32, lagged.shape, 1)
    inside = (lag >= window_ref[:, 0:1]) & (lag < window_ref[:, 1:2])
    residual = jnp.where(inside, lagged - observed_ref[...].astype(jnp.float32), 0.0)
    adjoint = jnp.dot(
        residual.astype(jnp.bfloat16), back_ref[...], preferred_element_type=jnp.float32
    )
    spec = cross[...].astype(jnp.float32)
    out_ref[...] = (
        adjoint[:, :half] * spec[:, :half] + adjoint[:, half:] * spec[:, half:]
    ).astype(jnp.bfloat16)


def sum_kernel(
    ids_ref, kernel_ref, out_ref,
    sums, side_send, side_recv, diag_send, diag_across, diag_along, far_send, far_recv,
    side_ss, side_rs, send_sem, recv_sem,
):
    me = lax.axis_index("pairs")
    across, along, diagonal, sibling = neighbours(me)
    stations, width = out_ref.shape
    half = stations // 2
    shift = 1 - 2 * (me % 2)

    barrier = pltpu.get_barrier_semaphore()
    for peer in (across, along, sibling):
        pl.semaphore_signal(barrier, inc=1, device_id={"pairs": peer}, device_id_type=MESH)
    pl.semaphore_wait(barrier, 3)

    def partial(owner, first):
        here = lax.broadcasted_iota(jnp.int32, (half, ids_ref.shape[1]), 0)
        base = owner * stations + first
        hit = (here == ids_ref[0:1, :] - base) | (here == ids_ref[1:2, :] - base)
        return jnp.dot(
            hit.astype(jnp.bfloat16), kernel_ref[...], preferred_element_type=jnp.float32
        )

    def send(src, dst, sem, target):
        copy = pltpu.make_async_remote_copy(
            src_ref=src, dst_ref=dst, send_sem=send_sem.at[sem], recv_sem=recv_sem.at[sem],
            device_id={"pairs": target}, device_id_type=MESH,
        )
        copy.start()
        return copy

    low, high = pl.ds(0, half), pl.ds(half, half)
    sides = []

    def chip_sum(q, chip):
        def other(i, carry):
            first = pl.multiple_of(i * half, half)
            side_send[q, pl.ds(first, half), :] = partial(chip + shift, first).astype(
                jnp.bfloat16
            )
            return carry

        lax.fori_loop(0, 2, other, 0)
        copy = pltpu.make_async_remote_copy(
            src_ref=side_send.at[q], dst_ref=side_recv.at[q], send_sem=side_ss.at[q],
            recv_sem=side_rs.at[q], device_id={"pairs": sibling}, device_id_type=MESH,
        )
        copy.start()
        sides.append(copy)

        def mine(i, carry):
            first = pl.multiple_of(i * half, half)
            sums[q, pl.ds(first, half), :] = partial(chip, first)
            return carry

        lax.fori_loop(0, 2, mine, 0)
        copy.wait_recv()

    def whole(q, rows):
        return sums[q, rows, :] + side_recv[q, rows, :].astype(jnp.float32)

    chip_sum(0, diagonal)
    diag_send[low, :] = whole(0, low).astype(jnp.bfloat16)
    to_across = send(diag_send.at[low], diag_across, 0, across)
    diag_send[high, :] = whole(0, high).astype(jnp.bfloat16)
    to_along = send(diag_send.at[high], diag_along, 1, along)

    chip_sum(1, across)
    far_send[0, low, :] = whole(1, low).astype(jnp.bfloat16)
    first_across = send(far_send.at[0, low], far_recv.at[0, low], 2, across)
    chip_sum(2, along)
    far_send[1, high, :] = whole(2, high).astype(jnp.bfloat16)
    first_along = send(far_send.at[1, high], far_recv.at[1, high], 3, along)

    to_along.wait_recv()
    far_send[0, high, :] = (whole(1, high) + diag_along[...].astype(jnp.float32)).astype(
        jnp.bfloat16
    )
    last_across = send(far_send.at[0, high], far_recv.at[0, high], 4, across)
    to_across.wait_recv()
    far_send[1, low, :] = (whole(2, low) + diag_across[...].astype(jnp.float32)).astype(
        jnp.bfloat16
    )
    last_along = send(far_send.at[1, low], far_recv.at[1, low], 5, along)

    chip_sum(3, me)
    for copy in (first_across, first_along, last_across, last_along):
        copy.wait_recv()
    for rows in (low, high):
        out_ref[rows, :] = 0.25 * (
            whole(3, rows)
            + far_recv[0, rows, :].astype(jnp.float32)
            + far_recv[1, rows, :].astype(jnp.float32)
        )
    for copy in (to_across, to_along, first_across, first_along, last_across, last_along):
        copy.wait_send()
    for copy in sides:
        copy.wait_send()


def chip_shards(spectra, observed, pair_owner, pair_slot, win_start, win_end):
    owners = lax.axis_size("pairs")
    bands = lax.axis_size("band")
    stations, _, width = spectra.shape
    half = width // 2
    pairs, _, lags = observed.shape
    tile = min(256, pairs)
    bf16, f32 = jnp.bfloat16, jnp.float32
    vmem = pl.BlockSpec(memory_space=pltpu.VMEM)
    hbm = pl.BlockSpec(memory_space=pl.ANY)
    dma = pltpu.SemaphoreType.DMA

    spectra = spectra.reshape(stations, width)
    observed = observed.reshape(pairs, lags)
    ids = (pair_owner * stations + pair_slot).astype(jnp.int32).T
    window = jnp.stack([win_start, win_end], axis=1)
    table = basis_constant(half, lags)

    with jax.named_scope("spread_spectra"):
        panel, scale = pl.pallas_call(
            functools.partial(gather_kernel, bands, bands * width, owners),
            out_shape=(
                jax.ShapeDtypeStruct((owners, stations, width), bf16),
                jax.ShapeDtypeStruct((owners, 8, stations), f32),
            ),
            in_specs=[vmem, hbm],
            out_specs=(hbm, vmem),
            scratch_shapes=[
                pltpu.VMEM((8, stations), f32),
                pltpu.VMEM((bands, 8, stations), f32),
                pltpu.VMEM((8, stations), f32),
                pltpu.VMEM((owners, 8, stations), f32),
                dma, dma((14,)), dma((14,)), dma((bands,)), dma((bands,)),
                dma((owners,)), dma((owners,)),
            ],
            compiler_params=pltpu.CompilerParams(
                collective_id=0, has_side_effects=True, vmem_limit_bytes=VMEM_LIMIT
            ),
        )(spectra, spectra)

    once = pl.Buffered(1)
    with jax.named_scope("pair_kernels"):
        kernels = pl.pallas_call(
            pair_kernel,
            out_shape=jax.ShapeDtypeStruct((pairs, half), bf16),
            grid_spec=pltpu.PrefetchScalarGridSpec(
                num_scalar_prefetch=1,
                grid=(pairs // tile,),
                in_specs=[
                    pl.BlockSpec(
                        (owners, stations, width), lambda i, s: (0, 0, 0), pipeline_mode=once
                    ),
                    pl.BlockSpec(
                        (owners, 8, stations), lambda i, s: (0, 0, 0), pipeline_mode=once
                    ),
                    pl.BlockSpec((tile, lags), lambda i, s: (i, 0)),
                    pl.BlockSpec((tile, 2), lambda i, s: (i, 0)),
                    pl.BlockSpec((width, lags), lambda i, s: (0, 0), pipeline_mode=once),
                    pl.BlockSpec((lags, width), lambda i, s: (0, 0), pipeline_mode=once),
                ],
                out_specs=pl.BlockSpec((tile, half), lambda i, s: (i, 0)),
                scratch_shapes=[
                    pltpu.VMEM((owners * stations * width // 128, 128), f32),
                    pltpu.VMEM((tile * width // 128, 128), f32),
                    pltpu.VMEM((tile * width // 128, 128), f32),
                    pltpu.VMEM((tile, width), bf16),
                ],
            ),
            compiler_params=pltpu.CompilerParams(vmem_limit_bytes=VMEM_LIMIT),
        )(
            (ids * (width // 128)).reshape(-1),
            panel,
            scale,
            observed,
            window,
            jnp.asarray(table, bf16),
            jnp.asarray(table.T, bf16),
        )

    with jax.named_scope("station_sums"):
        out = pl.pallas_call(
            sum_kernel,
            out_shape=jax.ShapeDtypeStruct((stations, half), f32),
            in_specs=[vmem, vmem],
            out_specs=vmem,
            scratch_shapes=[
                pltpu.VMEM((4, stations, half), f32),
                pltpu.VMEM((4, stations, half), bf16),
                pltpu.VMEM((4, stations, half), bf16),
                pltpu.VMEM((stations, half), bf16),
                pltpu.VMEM((stations // 2, half), bf16),
                pltpu.VMEM((stations // 2, half), bf16),
                pltpu.VMEM((2, stations, half), bf16),
                pltpu.VMEM((2, stations, half), bf16),
                dma((4,)), dma((4,)), dma((6,)), dma((6,)),
            ],
            compiler_params=pltpu.CompilerParams(
                collective_id=1, has_side_effects=True, vmem_limit_bytes=VMEM_LIMIT
            ),
        )(ids, kernels)
    return out.reshape(stations, 1, half)


def lag_basis(half_width, lag_count):
    freqs = jnp.arange(half_width, dtype=jnp.int32)
    lag_index = jnp.arange(lag_count, dtype=jnp.int32)
    phases = (freqs[:, None] * lag_index[None, :] % lag_count).astype(jnp.float32) * (
        2.0 * math.pi / lag_count
    )
    factor = 1.0 / math.sqrt(lag_count)
    return jnp.concatenate([jnp.cos(phases) * factor, -jnp.sin(phases) * factor], axis=0).astype(
        jnp.bfloat16
    )


def owner_positions(owner_flat, owner_count):
    onehot = (owner_flat[:, None] == jnp.arange(owner_count, dtype=jnp.int32)[None, :]).astype(
        jnp.int32
    )
    before = jnp.cumsum(onehot, axis=0) - onehot
    return jnp.sum(before * onehot, axis=1)


def shards(spectra, observed, pair_owner, pair_slot, win_start, win_end):
    owners = lax.axis_size("pairs")
    station_count = spectra.shape[0]
    band_count = spectra.shape[1]
    full_width = spectra.shape[2]
    half_width = full_width // 2
    pair_count = observed.shape[0]
    lag_count = observed.shape[2]
    capacity = 3 * pair_count // owners
    spectrum = spectra.astype(jnp.float32)
    local_power = jnp.sum(spectrum * spectrum, axis=(1, 2))
    total_power = lax.psum(local_power, "band")
    entries = band_count * lax.axis_size("band") * full_width
    whitened = (spectrum * lax.rsqrt(total_power / entries + 1e-05)[:, None, None]).astype(
        jnp.bfloat16
    )
    owner_flat = pair_owner.reshape(-1)
    slot_flat = pair_slot.reshape(-1)
    position = owner_positions(owner_flat, owners)
    request = (
        jnp.full((owners, capacity), station_count, jnp.int32)
        .at[owner_flat, position]
        .set(slot_flat)
    )
    wanted = lax.all_to_all(request, "pairs", split_axis=0, concat_axis=0, tiled=True)
    panel_rows = lax.all_gather(whitened, "pairs", axis=0, tiled=True)
    fetched = panel_rows[owner_flat * station_count + slot_flat]
    fetched = fetched.reshape(pair_count, 2, band_count, full_width)
    near_end = fetched[:, 0].astype(jnp.float32)
    far_end = fetched[:, 1].astype(jnp.float32)
    near_re, near_im = (near_end[..., :half_width], near_end[..., half_width:])
    far_re, far_im = (far_end[..., :half_width], far_end[..., half_width:])
    cross_spec = jnp.concatenate(
        [near_re * far_re + near_im * far_im, near_im * far_re - near_re * far_im], axis=-1
    ).astype(jnp.bfloat16)
    table = lag_basis(half_width, lag_count)
    lagged = jnp.einsum("pbf,ft->pbt", cross_spec, table, preferred_element_type=jnp.float32)
    lag_index = jnp.arange(lag_count, dtype=jnp.int32)
    window = (
        (lag_index[None, :] >= win_start[:, None]) & (lag_index[None, :] < win_end[:, None])
    ).astype(jnp.float32)
    residual = (window[:, None, :] * (lagged - observed.astype(jnp.float32))).astype(jnp.bfloat16)
    adjoint = jnp.einsum("pbt,ft->pbf", residual, table, preferred_element_type=jnp.float32)
    adj_re, adj_im = (adjoint[..., :half_width], adjoint[..., half_width:])
    to_first = jnp.concatenate(
        [adj_re * far_re - adj_im * far_im, adj_re * far_im + adj_im * far_re], axis=-1
    ).astype(jnp.bfloat16)
    to_second = jnp.concatenate(
        [adj_re * near_re + adj_im * near_im, adj_re * near_im - adj_im * near_re], axis=-1
    ).astype(jnp.bfloat16)
    stacked = jnp.stack([to_first, to_second], axis=1).reshape(
        2 * pair_count, band_count, full_width
    )
    outgoing = (
        jnp.zeros((owners, capacity, band_count, full_width), jnp.bfloat16)
        .at[owner_flat, position]
        .set(stacked)
    )
    incoming = lax.all_to_all(outgoing, "pairs", split_axis=0, concat_axis=0, tiled=True)

    def add_source(source, summed):
        block_rows = lax.dynamic_index_in_dim(incoming, source, 0, keepdims=False).astype(
            jnp.float32
        )
        block_ids = lax.dynamic_index_in_dim(wanted, source, 0, keepdims=False)
        return summed.at[block_ids].add(block_rows)

    summed = lax.fori_loop(
        0, owners, add_source, jnp.zeros((station_count + 1, band_count, full_width), jnp.float32)
    )
    summed = summed[:station_count]
    own_spec = whitened.astype(jnp.float32)
    return 0.25 * (
        summed[..., :half_width] * own_spec[..., :half_width]
        + summed[..., half_width:] * own_spec[..., half_width:]
    )


def solution(mesh):
    square_of_chips = mesh.shape["pairs"] == 8
    return jax.shard_map(
        chip_shards if square_of_chips else shards,
        mesh=mesh,
        in_specs=(
            P("pairs", "band", None),
            P("pairs", "band", None),
            P("pairs", None),
            P("pairs", None),
            P("pairs"),
            P("pairs"),
        ),
        out_specs=P("pairs", "band", None),
        check_vma=False,
    )
```

```python
import functools
import math

import jax
import jax.numpy as jnp
import numpy as np
from jax import lax
from jax.experimental import pallas as pl
from jax.experimental.pallas import tpu as pltpu
from jax.sharding import PartitionSpec as P

MESH = pl.DeviceIdType.MESH
VMEM_LIMIT = 60 * 1024 * 1024


def basis_constant(half_width, lag_count):
    phases = (np.arange(half_width)[:, None] * np.arange(lag_count)[None, :] % lag_count) * (
        2.0 * math.pi / lag_count
    )
    factor = 1.0 / math.sqrt(lag_count)
    table = np.concatenate([np.cos(phases) * factor, -np.sin(phases) * factor], axis=0)
    return table.astype(np.float32)


def neighbours(me):
    core, x, y = me % 2, (me // 2) % 2, me // 4
    across, along = me + 2 - 4 * x, me + 4 - 8 * y
    return across, along, across + 4 - 8 * y, me + 1 - 2 * core


def pair_kernel(
    bands, owners, tile,
    spec_ref, ids_ref, start_ref, end_ref, observed_hbm, table_hbm, back_hbm, out_ref,
    arr, panel, near, far, cross, lagged, observed, table, back, edges,
    part, part_recv, total, total_recv,
    local_sem, send_sem, recv_sem, band_send, band_recv, total_send, total_recv_sem,
):
    me = lax.axis_index("pairs")
    band = lax.axis_index("band")
    across, along, diagonal, sibling = neighbours(me)
    shift = 1 - 2 * (me % 2)
    stations, width = spec_ref.shape
    pairs, lags = observed.shape
    piece = width // 2
    bins = piece // 2
    groups = width // 128
    fold = groups // 4
    half = stations // 2
    chunk = 64
    names = {}
    panel_rows = panel.reshape(owners * stations * groups, 128)

    barrier = pltpu.get_barrier_semaphore()
    for k in range(1, owners):
        pl.semaphore_signal(
            barrier, inc=1, device_id={"pairs": lax.rem(me + k, owners)}, device_id_type=MESH
        )
    for k in range(1, bands):
        pl.semaphore_signal(
            barrier, inc=1, device_id={"band": lax.rem(band + k, bands)}, device_id_type=MESH
        )
    loads = []
    for source, target in ((table_hbm, table), (back_hbm, back), (observed_hbm, observed)):
        loads.append(pltpu.make_async_copy(source, target, local_sem.at[len(loads)]))
        loads[-1].start()
    for h in range(2):
        arr[h, me, :, 0:bins] = spec_ref[:, h * bins : h * bins + bins]
        arr[h, me, :, bins:piece] = spec_ref[:, piece + h * bins : piece + h * bins + bins]
    pl.semaphore_wait(barrier, owners + bands - 2)

    sent = []

    def transfer(h, owner, rows, key, target):
        place = arr.at[h, owner] if rows is None else arr.at[h, owner, pl.ds(rows * half, half)]
        sem = names.setdefault((key, h, rows), len(names))
        return pltpu.make_async_remote_copy(
            src_ref=place, dst_ref=place, send_sem=send_sem.at[sem], recv_sem=recv_sem.at[sem],
            device_id={"pairs": target}, device_id_type=MESH,
        )

    def push(*message):
        sent.append(transfer(*message))
        sent[-1].start()

    def arrived(h, owner, rows, key):
        transfer(h, owner, rows, key, sibling).wait_recv()

    def push_own(h):
        push(h, me, 0, "x", across)
        push(h, me, 1, "y", along)
        push(h, me, 1, "x", across)
        push(h, me, 0, "y", along)
        push(h, me, None, "own", sibling)

    def forward(h):
        arrived(h, across, 0, "x")
        push(h, across, 0, "diagonal", along)
        arrived(h, along, 1, "y")
        push(h, along, 1, "diagonal", across)

    def whiten(h, o):
        scale = total_recv[o].T[:, 0:1]
        for r in range(0, stations, chunk):
            rows = arr[h, o, r : r + chunk, :].astype(jnp.float32) * scale[r : r + chunk]
            rows = rows.astype(jnp.bfloat16).astype(jnp.float32)
            for j in range(groups // 2):
                first = (o * stations + r) * groups + h * (groups // 2) + j
                panel_rows[pl.ds(first, chunk, stride=groups), :] = rows[
                    :, j * 128 : j * 128 + 128
                ]

    def share(h):
        arrived(h, across, 1, "x")
        push(h, across, None, "over x", sibling)
        arrived(h, along, 0, "y")
        push(h, along, None, "over y", sibling)
        whiten(h, across)
        whiten(h, along)
        arrived(h, me + shift, None, "own")
        whiten(h, me + shift)

    def finish(h):
        arrived(h, diagonal, 0, "diagonal")
        arrived(h, diagonal, 1, "diagonal")
        push(h, diagonal, None, "over both", sibling)
        arrived(h, across + shift, None, "over x")
        whiten(h, across + shift)
        arrived(h, along + shift, None, "over y")
        whiten(h, along + shift)
        whiten(h, diagonal)
        arrived(h, diagonal + shift, None, "over both")
        whiten(h, diagonal + shift)

    push_own(0)

    spectrum = spec_ref[...].astype(jnp.float32)
    square = spectrum * spectrum
    upper = square.astype(jnp.bfloat16)
    lower = (square - upper.astype(jnp.float32)).astype(jnp.bfloat16)
    ones = jnp.ones((8, width), jnp.bfloat16)
    dims = (((1,), (1,)), ((), ()))
    part[...] = lax.dot_general(
        ones, upper, dims, preferred_element_type=jnp.float32
    ) + lax.dot_general(ones, lower, dims, preferred_element_type=jnp.float32)
    copies = []
    for k in range(1, bands):
        copies.append(
            pltpu.make_async_remote_copy(
                src_ref=part, dst_ref=part_recv.at[k], send_sem=band_send.at[k],
                recv_sem=band_recv.at[k],
                device_id={"band": lax.rem(band + k, bands)}, device_id_type=MESH,
            )
        )
        copies[-1].start()
    for copy in copies:
        copy.wait()
    power = part[...]
    for k in range(1, bands):
        power = power + part_recv[k]
    total[...] = lax.rsqrt(power / (bands * width) + 1e-05)
    total_recv[me] = total[...]
    copies = []
    for k in range(1, owners):
        copies.append(
            pltpu.make_async_remote_copy(
                src_ref=total, dst_ref=total_recv.at[me], send_sem=total_send.at[k],
                recv_sem=total_recv_sem.at[k],
                device_id={"pairs": lax.rem(me + k, owners)}, device_id_type=MESH,
            )
        )
        copies[-1].start()
    for t in range(0, pairs, tile):
        for side, source in enumerate((start_ref, end_ref)):
            column = jnp.broadcast_to(source[0:1, t : t + tile], (8, tile)).T
            edges[t : t + tile, side : side + 1] = column[:, 0:1]
    whiten(0, me)
    for copy in copies:
        copy.wait()

    def fetch_tile(h, t):
        def fetch(i, carry):
            for u in range(16):
                p = i * 16 + u
                here = pl.ds(pl.multiple_of(p * groups, groups), groups)
                near[here, :] = panel[ids_ref[0, t * tile + p]]
                far[here, :] = panel[ids_ref[1, t * tile + p]]
            return carry

        lax.fori_loop(0, tile // 16, fetch, 0)

        def multiply(i, carry):
            rows = pl.ds(pl.multiple_of(t * tile + i * chunk, chunk), chunk)
            for j in range(fold):
                first = i * chunk * groups + h * (groups // 2) + j
                re = pl.ds(first, chunk, stride=groups)
                im = pl.ds(first + fold, chunk, stride=groups)
                ar, ai, br, bi = near[re, :], near[im, :], far[re, :], far[im, :]
                cross[h, rows, j * 128 : j * 128 + 128] = (ar * br + ai * bi).astype(jnp.bfloat16)
                cross[h, rows, bins + j * 128 : bins + j * 128 + 128] = (
                    ai * br - ar * bi
                ).astype(jnp.bfloat16)
            return carry

        lax.fori_loop(0, tile // chunk, multiply, 0)

    def first_piece(t, carry):
        rows = pl.ds(pl.multiple_of(t * tile, tile), tile)
        fetch_tile(0, t)
        lagged[rows, :] = jnp.dot(
            cross[0, rows, :], table[0:piece, :], preferred_element_type=jnp.float32
        )
        return carry

    def second_piece(t, carry):
        rows = pl.ds(pl.multiple_of(t * tile, tile), tile)
        fetch_tile(1, t)
        sums = lagged[rows, :] + jnp.dot(
            cross[1, rows, :], table[piece:width, :], preferred_element_type=jnp.float32
        )
        lag = lax.broadcasted_iota(jnp.int32, sums.shape, 1)
        inside = (lag >= edges[rows, 0:1]) & (lag < edges[rows, 1:2])
        residual = jnp.where(inside, sums - observed[rows, :].astype(jnp.float32), 0.0)
        residual = residual.astype(jnp.bfloat16)
        for h in range(2):
            adjoint = jnp.dot(
                residual,
                back[:, h * piece : h * piece + piece],
                preferred_element_type=jnp.float32,
            )
            spec = cross[h, rows, :].astype(jnp.float32)
            out_ref[rows, h * bins : h * bins + bins] = (
                adjoint[:, :bins] * spec[:, :bins] + adjoint[:, bins:] * spec[:, bins:]
            ).astype(jnp.bfloat16)
        return carry

    tiles = pairs // tile
    forward(0)
    push_own(1)
    share(0)
    finish(0)
    for copy in loads:
        copy.wait()
    lax.fori_loop(0, tiles // 2, first_piece, 0)
    forward(1)
    lax.fori_loop(tiles // 2, tiles, first_piece, 0)
    whiten(1, me)
    share(1)
    finish(1)
    lax.fori_loop(0, tiles, second_piece, 0)
    for copy in sent:
        copy.wait_send()


def sum_kernel(
    stations, owner_ref, slot_ref, kernel_ref, out_ref,
    sums, side_send, side_recv, diag_send, diag_across, diag_along, far_send, far_recv,
    side_ss, side_rs, send_sem, recv_sem,
):
    me = lax.axis_index("pairs")
    across, along, diagonal, sibling = neighbours(me)
    groups = kernel_ref.shape[1] // 128
    half = stations // 2
    shift = 1 - 2 * (me % 2)

    barrier = pltpu.get_barrier_semaphore()
    for peer in (across, along, sibling):
        pl.semaphore_signal(barrier, inc=1, device_id={"pairs": peer}, device_id_type=MESH)
    pl.semaphore_wait(barrier, 3)

    def partial(owner, first):
        here = lax.broadcasted_iota(jnp.int32, (half, slot_ref.shape[1]), 0)
        place = jnp.where(owner_ref[...] == owner, slot_ref[...] - first, -1)
        hit = (here == place[0:1, :]) | (here == place[1:2, :])
        return jnp.dot(
            hit.astype(jnp.bfloat16), kernel_ref[...], preferred_element_type=jnp.float32
        )

    def send(src, dst, sem, target):
        copy = pltpu.make_async_remote_copy(
            src_ref=src, dst_ref=dst, send_sem=send_sem.at[sem], recv_sem=recv_sem.at[sem],
            device_id={"pairs": target}, device_id_type=MESH,
        )
        copy.start()
        return copy

    low, high = pl.ds(0, half), pl.ds(half, half)
    sides = []

    def chip_sum(q, chip):
        def other(i, carry):
            first = pl.multiple_of(i * half, half)
            side_send[q, pl.ds(first, half), :] = partial(chip + shift, first).astype(
                jnp.bfloat16
            )
            return carry

        lax.fori_loop(0, 2, other, 0)
        copy = pltpu.make_async_remote_copy(
            src_ref=side_send.at[q], dst_ref=side_recv.at[q], send_sem=side_ss.at[q],
            recv_sem=side_rs.at[q], device_id={"pairs": sibling}, device_id_type=MESH,
        )
        copy.start()
        sides.append(copy)

        def mine(i, carry):
            first = pl.multiple_of(i * half, half)
            sums[q, pl.ds(first, half), :] = partial(chip, first)
            return carry

        lax.fori_loop(0, 2, mine, 0)
        copy.wait_recv()

    def whole(q, rows):
        return sums[q, rows, :] + side_recv[q, rows, :].astype(jnp.float32)

    chip_sum(0, diagonal)
    diag_send[low, :] = whole(0, low).astype(jnp.bfloat16)
    to_across = send(diag_send.at[low], diag_across, 0, across)
    diag_send[high, :] = whole(0, high).astype(jnp.bfloat16)
    to_along = send(diag_send.at[high], diag_along, 1, along)

    chip_sum(1, across)
    far_send[0, low, :] = whole(1, low).astype(jnp.bfloat16)
    first_across = send(far_send.at[0, low], far_recv.at[0, low], 2, across)
    chip_sum(2, along)
    far_send[1, high, :] = whole(2, high).astype(jnp.bfloat16)
    first_along = send(far_send.at[1, high], far_recv.at[1, high], 3, along)

    to_along.wait_recv()
    far_send[0, high, :] = (whole(1, high) + diag_along[...].astype(jnp.float32)).astype(
        jnp.bfloat16
    )
    last_across = send(far_send.at[0, high], far_recv.at[0, high], 4, across)
    to_across.wait_recv()
    far_send[1, low, :] = (whole(2, low) + diag_across[...].astype(jnp.float32)).astype(
        jnp.bfloat16
    )
    last_along = send(far_send.at[1, low], far_recv.at[1, low], 5, along)

    chip_sum(3, me)
    for copy in (first_across, first_along, last_across, last_along):
        copy.wait_recv()
    for first in (0, half):
        rows = pl.ds(first, half)
        result = 0.25 * (
            whole(3, rows)
            + far_recv[0, rows, :].astype(jnp.float32)
            + far_recv[1, rows, :].astype(jnp.float32)
        )
        for j in range(groups):
            out_ref[pl.ds(first * groups + j, half, stride=groups), :] = result[
                :, j * 128 : j * 128 + 128
            ]
    for copy in (to_across, to_along, first_across, first_along, last_across, last_along):
        copy.wait_send()
    for copy in sides:
        copy.wait_send()


def chip_shards(spectra, observed, pair_owner, pair_slot, win_start, win_end):
    owners = lax.axis_size("pairs")
    bands = lax.axis_size("band")
    stations, _, width = spectra.shape
    half = width // 2
    pairs, _, lags = observed.shape
    tile = min(256, pairs)
    bf16, f32 = jnp.bfloat16, jnp.float32
    vmem = pl.BlockSpec(memory_space=pltpu.VMEM)
    hbm = pl.BlockSpec(memory_space=pl.ANY)
    dma = pltpu.SemaphoreType.DMA

    table = basis_constant(half, lags).reshape(2, 2, half // 2, lags)
    table = table.transpose(1, 0, 2, 3).reshape(width, lags)
    owner_rows, slot_rows = pair_owner.T, pair_slot.T

    with jax.named_scope("pair_kernels"):
        kernels = pl.pallas_call(
            functools.partial(pair_kernel, bands, owners, tile),
            out_shape=jax.ShapeDtypeStruct((pairs, half), bf16),
            in_specs=[vmem, pl.BlockSpec(memory_space=pltpu.SMEM), vmem, vmem] + [hbm] * 3,
            out_specs=vmem,
            scratch_shapes=[
                pltpu.VMEM((2, owners, stations, half), bf16),
                pltpu.VMEM((owners * stations, width // 128, 128), f32),
                pltpu.VMEM((tile * width // 128, 128), f32),
                pltpu.VMEM((tile * width // 128, 128), f32),
                pltpu.VMEM((2, pairs, half), bf16),
                pltpu.VMEM((pairs, lags), f32),
                pltpu.VMEM((pairs, lags), bf16),
                pltpu.VMEM((width, lags), bf16),
                pltpu.VMEM((lags, width), bf16),
                pltpu.VMEM((pairs, 2), jnp.int32),
                pltpu.VMEM((8, stations), f32),
                pltpu.VMEM((bands, 8, stations), f32),
                pltpu.VMEM((8, stations), f32),
                pltpu.VMEM((owners, 8, stations), f32),
                dma((3,)), dma((20,)), dma((20,)), dma((bands,)), dma((bands,)),
                dma((owners,)), dma((owners,)),
            ],
            compiler_params=pltpu.CompilerParams(
                collective_id=0, has_side_effects=True, vmem_limit_bytes=VMEM_LIMIT
            ),
        )(
            spectra.reshape(stations, width),
            owner_rows * stations + slot_rows,
            win_start.reshape(1, pairs),
            win_end.reshape(1, pairs),
            observed.reshape(pairs, lags),
            jnp.asarray(table, bf16),
            jnp.asarray(table.T, bf16),
        )

    with jax.named_scope("station_sums"):
        out = pl.pallas_call(
            functools.partial(sum_kernel, stations),
            out_shape=jax.ShapeDtypeStruct((stations * half // 128, 128), f32),
            in_specs=[vmem] * 3,
            out_specs=vmem,
            scratch_shapes=[
                pltpu.VMEM((4, stations, half), f32),
                pltpu.VMEM((4, stations, half), bf16),
                pltpu.VMEM((4, stations, half), bf16),
                pltpu.VMEM((stations, half), bf16),
                pltpu.VMEM((stations // 2, half), bf16),
                pltpu.VMEM((stations // 2, half), bf16),
                pltpu.VMEM((2, stations, half), bf16),
                pltpu.VMEM((2, stations, half), bf16),
                dma((4,)), dma((4,)), dma((6,)), dma((6,)),
            ],
            compiler_params=pltpu.CompilerParams(
                collective_id=1, has_side_effects=True, vmem_limit_bytes=VMEM_LIMIT
            ),
        )(owner_rows, slot_rows, kernels)
    return out.reshape(stations, 1, half)


def lag_basis(half_width, lag_count):
    freqs = jnp.arange(half_width, dtype=jnp.int32)
    lag_index = jnp.arange(lag_count, dtype=jnp.int32)
    phases = (freqs[:, None] * lag_index[None, :] % lag_count).astype(jnp.float32) * (
        2.0 * math.pi / lag_count
    )
    factor = 1.0 / math.sqrt(lag_count)
    return jnp.concatenate([jnp.cos(phases) * factor, -jnp.sin(phases) * factor], axis=0).astype(
        jnp.bfloat16
    )


def owner_positions(owner_flat, owner_count):
    onehot = (owner_flat[:, None] == jnp.arange(owner_count, dtype=jnp.int32)[None, :]).astype(
        jnp.int32
    )
    before = jnp.cumsum(onehot, axis=0) - onehot
    return jnp.sum(before * onehot, axis=1)


def shards(spectra, observed, pair_owner, pair_slot, win_start, win_end):
    owners = lax.axis_size("pairs")
    station_count = spectra.shape[0]
    band_count = spectra.shape[1]
    full_width = spectra.shape[2]
    half_width = full_width // 2
    pair_count = observed.shape[0]
    lag_count = observed.shape[2]
    capacity = 3 * pair_count // owners
    spectrum = spectra.astype(jnp.float32)
    local_power = jnp.sum(spectrum * spectrum, axis=(1, 2))
    total_power = lax.psum(local_power, "band")
    entries = band_count * lax.axis_size("band") * full_width
    whitened = (spectrum * lax.rsqrt(total_power / entries + 1e-05)[:, None, None]).astype(
        jnp.bfloat16
    )
    owner_flat = pair_owner.reshape(-1)
    slot_flat = pair_slot.reshape(-1)
    position = owner_positions(owner_flat, owners)
    request = (
        jnp.full((owners, capacity), station_count, jnp.int32)
        .at[owner_flat, position]
        .set(slot_flat)
    )
    wanted = lax.all_to_all(request, "pairs", split_axis=0, concat_axis=0, tiled=True)
    panel_rows = lax.all_gather(whitened, "pairs", axis=0, tiled=True)
    fetched = panel_rows[owner_flat * station_count + slot_flat]
    fetched = fetched.reshape(pair_count, 2, band_count, full_width)
    near_end = fetched[:, 0].astype(jnp.float32)
    far_end = fetched[:, 1].astype(jnp.float32)
    near_re, near_im = (near_end[..., :half_width], near_end[..., half_width:])
    far_re, far_im = (far_end[..., :half_width], far_end[..., half_width:])
    cross_spec = jnp.concatenate(
        [near_re * far_re + near_im * far_im, near_im * far_re - near_re * far_im], axis=-1
    ).astype(jnp.bfloat16)
    table = lag_basis(half_width, lag_count)
    lagged = jnp.einsum("pbf,ft->pbt", cross_spec, table, preferred_element_type=jnp.float32)
    lag_index = jnp.arange(lag_count, dtype=jnp.int32)
    window = (
        (lag_index[None, :] >= win_start[:, None]) & (lag_index[None, :] < win_end[:, None])
    ).astype(jnp.float32)
    residual = (window[:, None, :] * (lagged - observed.astype(jnp.float32))).astype(jnp.bfloat16)
    adjoint = jnp.einsum("pbt,ft->pbf", residual, table, preferred_element_type=jnp.float32)
    adj_re, adj_im = (adjoint[..., :half_width], adjoint[..., half_width:])
    to_first = jnp.concatenate(
        [adj_re * far_re - adj_im * far_im, adj_re * far_im + adj_im * far_re], axis=-1
    ).astype(jnp.bfloat16)
    to_second = jnp.concatenate(
        [adj_re * near_re + adj_im * near_im, adj_re * near_im - adj_im * near_re], axis=-1
    ).astype(jnp.bfloat16)
    stacked = jnp.stack([to_first, to_second], axis=1).reshape(
        2 * pair_count, band_count, full_width
    )
    outgoing = (
        jnp.zeros((owners, capacity, band_count, full_width), jnp.bfloat16)
        .at[owner_flat, position]
        .set(stacked)
    )
    incoming = lax.all_to_all(outgoing, "pairs", split_axis=0, concat_axis=0, tiled=True)

    def add_source(source, summed):
        block_rows = lax.dynamic_index_in_dim(incoming, source, 0, keepdims=False).astype(
            jnp.float32
        )
        block_ids = lax.dynamic_index_in_dim(wanted, source, 0, keepdims=False)
        return summed.at[block_ids].add(block_rows)

    summed = lax.fori_loop(
        0, owners, add_source, jnp.zeros((station_count + 1, band_count, full_width), jnp.float32)
    )
    summed = summed[:station_count]
    own_spec = whitened.astype(jnp.float32)
    return 0.25 * (
        summed[..., :half_width] * own_spec[..., :half_width]
        + summed[..., half_width:] * own_spec[..., half_width:]
    )


def solution(mesh):
    square_of_chips = mesh.shape["pairs"] == 8
    return jax.shard_map(
        chip_shards if square_of_chips else shards,
        mesh=mesh,
        in_specs=(
            P("pairs", "band", None),
            P("pairs", "band", None),
            P("pairs", None),
            P("pairs", None),
            P("pairs"),
            P("pairs"),
        ),
        out_specs=P("pairs", "band", None),
        check_vma=False,
    )
```

```python
import functools
import math

import jax
import jax.numpy as jnp
import numpy as np
from jax import lax
from jax.experimental import pallas as pl
from jax.experimental.pallas import tpu as pltpu
from jax.sharding import PartitionSpec as P

MESH = pl.DeviceIdType.MESH
VMEM_LIMIT = 60 * 1024 * 1024


def basis_constant(half_width, lag_count):
    phases = (np.arange(half_width)[:, None] * np.arange(lag_count)[None, :] % lag_count) * (
        2.0 * math.pi / lag_count
    )
    factor = 1.0 / math.sqrt(lag_count)
    table = np.concatenate([np.cos(phases) * factor, -np.sin(phases) * factor], axis=0)
    return table.astype(np.float32)


def neighbours(me):
    core, x, y = me % 2, (me // 2) % 2, me // 4
    across, along = me + 2 - 4 * x, me + 4 - 8 * y
    return across, along, across + 4 - 8 * y, me + 1 - 2 * core


def pair_kernel(
    bands, owners, tile,
    spec_ref, ids_ref, start_ref, end_ref, observed_hbm, table_hbm, back_hbm, out_ref,
    arr, panel, near, far, cross, lagged, observed, table, back, edges,
    part, part_recv, total, total_recv,
    local_sem, send_sem, recv_sem, band_send, band_recv, total_send, total_recv_sem,
):
    me = lax.axis_index("pairs")
    band = lax.axis_index("band")
    across, along, diagonal, sibling = neighbours(me)
    shift = 1 - 2 * (me % 2)
    stations, width = spec_ref.shape
    pairs, lags = observed.shape
    piece = width // 2
    bins = piece // 2
    groups = width // 128
    fold = groups // 4
    half = stations // 2
    chunk = 64
    names = {}
    panel_rows = panel.reshape(owners * stations * groups, 128)

    barrier = pltpu.get_barrier_semaphore()
    for k in range(1, owners):
        pl.semaphore_signal(
            barrier, inc=1, device_id={"pairs": lax.rem(me + k, owners)}, device_id_type=MESH
        )
    for k in range(1, bands):
        pl.semaphore_signal(
            barrier, inc=1, device_id={"band": lax.rem(band + k, bands)}, device_id_type=MESH
        )
    loads = []
    for source, target in ((table_hbm, table), (back_hbm, back), (observed_hbm, observed)):
        loads.append(pltpu.make_async_copy(source, target, local_sem.at[len(loads)]))
        loads[-1].start()
    for h in range(2):
        arr[h, me, :, 0:bins] = spec_ref[:, h * bins : h * bins + bins]
        arr[h, me, :, bins:piece] = spec_ref[:, piece + h * bins : piece + h * bins + bins]
    pl.semaphore_wait(barrier, owners + bands - 2)

    sent = []

    def transfer(h, owner, rows, key, target):
        place = arr.at[h, owner] if rows is None else arr.at[h, owner, pl.ds(rows * half, half)]
        sem = names.setdefault((key, h, rows), len(names))
        return pltpu.make_async_remote_copy(
            src_ref=place, dst_ref=place, send_sem=send_sem.at[sem], recv_sem=recv_sem.at[sem],
            device_id={"pairs": target}, device_id_type=MESH,
        )

    def push(*message):
        sent.append(transfer(*message))
        sent[-1].start()

    def arrived(h, owner, rows, key):
        transfer(h, owner, rows, key, sibling).wait_recv()

    def push_own(h):
        push(h, me, 0, "x", across)
        push(h, me, 1, "y", along)
        push(h, me, 1, "x", across)
        push(h, me, 0, "y", along)
        push(h, me, None, "own", sibling)

    def forward(h):
        arrived(h, across, 0, "x")
        push(h, across, 0, "diagonal", along)
        arrived(h, along, 1, "y")
        push(h, along, 1, "diagonal", across)

    def whiten(h, o):
        scale = total_recv[o].T[:, 0:1]
        for r in range(0, stations, chunk):
            rows = arr[h, o, r : r + chunk, :].astype(jnp.float32) * scale[r : r + chunk]
            rows = rows.astype(jnp.bfloat16).astype(jnp.float32)
            for j in range(groups // 2):
                first = (o * stations + r) * groups + h * (groups // 2) + j
                panel_rows[pl.ds(first, chunk, stride=groups), :] = rows[
                    :, j * 128 : j * 128 + 128
                ]

    def share(h):
        arrived(h, across, 1, "x")
        push(h, across, None, "over x", sibling)
        arrived(h, along, 0, "y")
        push(h, along, None, "over y", sibling)
        whiten(h, across)
        whiten(h, along)
        arrived(h, me + shift, None, "own")
        whiten(h, me + shift)

    def finish(h):
        arrived(h, diagonal, 0, "diagonal")
        arrived(h, diagonal, 1, "diagonal")
        push(h, diagonal, None, "over both", sibling)
        arrived(h, across + shift, None, "over x")
        whiten(h, across + shift)
        arrived(h, along + shift, None, "over y")
        whiten(h, along + shift)
        whiten(h, diagonal)
        arrived(h, diagonal + shift, None, "over both")
        whiten(h, diagonal + shift)

    push_own(0)

    spectrum = spec_ref[...].astype(jnp.float32)
    square = spectrum * spectrum
    upper = square.astype(jnp.bfloat16)
    lower = (square - upper.astype(jnp.float32)).astype(jnp.bfloat16)
    ones = jnp.ones((8, width), jnp.bfloat16)
    dims = (((1,), (1,)), ((), ()))
    part[...] = lax.dot_general(
        ones, upper, dims, preferred_element_type=jnp.float32
    ) + lax.dot_general(ones, lower, dims, preferred_element_type=jnp.float32)
    copies = []
    for k in range(1, bands):
        copies.append(
            pltpu.make_async_remote_copy(
                src_ref=part, dst_ref=part_recv.at[k], send_sem=band_send.at[k],
                recv_sem=band_recv.at[k],
                device_id={"band": lax.rem(band + k, bands)}, device_id_type=MESH,
            )
        )
        copies[-1].start()
    for copy in copies:
        copy.wait()
    power = part[...]
    for k in range(1, bands):
        power = power + part_recv[k]
    total[...] = lax.rsqrt(power / (bands * width) + 1e-05)
    total_recv[me] = total[...]
    copies = []
    for k in range(1, owners):
        copies.append(
            pltpu.make_async_remote_copy(
                src_ref=total, dst_ref=total_recv.at[me], send_sem=total_send.at[k],
                recv_sem=total_recv_sem.at[k],
                device_id={"pairs": lax.rem(me + k, owners)}, device_id_type=MESH,
            )
        )
        copies[-1].start()
    for t in range(0, pairs, tile):
        for side, source in enumerate((start_ref, end_ref)):
            column = jnp.broadcast_to(source[0:1, t : t + tile], (8, tile)).T
            edges[t : t + tile, side : side + 1] = column[:, 0:1]
    whiten(0, me)
    for copy in copies:
        copy.wait()

    def fetch_tile(h, t):
        def fetch(i, carry):
            for u in range(16):
                p = i * 16 + u
                here = pl.ds(pl.multiple_of(p * groups, groups), groups)
                near[here, :] = panel[ids_ref[0, t * tile + p]]
                far[here, :] = panel[ids_ref[1, t * tile + p]]
            return carry

        lax.fori_loop(0, tile // 16, fetch, 0)

        def multiply(i, carry):
            rows = pl.ds(pl.multiple_of(t * tile + i * chunk, chunk), chunk)
            for j in range(fold):
                first = i * chunk * groups + h * (groups // 2) + j
                re = pl.ds(first, chunk, stride=groups)
                im = pl.ds(first + fold, chunk, stride=groups)
                ar, ai, br, bi = near[re, :], near[im, :], far[re, :], far[im, :]
                cross[h, rows, j * 128 : j * 128 + 128] = (ar * br + ai * bi).astype(jnp.bfloat16)
                cross[h, rows, bins + j * 128 : bins + j * 128 + 128] = (
                    ai * br - ar * bi
                ).astype(jnp.bfloat16)
            return carry

        lax.fori_loop(0, tile // chunk, multiply, 0)

    def first_piece(t, carry):
        rows = pl.ds(pl.multiple_of(t * tile, tile), tile)
        fetch_tile(0, t)
        lagged[rows, :] = jnp.dot(
            cross[0, rows, :], table[0:piece, :], preferred_element_type=jnp.float32
        )
        return carry

    def second_piece(t, carry):
        rows = pl.ds(pl.multiple_of(t * tile, tile), tile)
        fetch_tile(1, t)
        sums = lagged[rows, :] + jnp.dot(
            cross[1, rows, :], table[piece:width, :], preferred_element_type=jnp.float32
        )
        lag = lax.broadcasted_iota(jnp.int32, sums.shape, 1)
        inside = (lag >= edges[rows, 0:1]) & (lag < edges[rows, 1:2])
        residual = jnp.where(inside, sums - observed[rows, :].astype(jnp.float32), 0.0)
        residual = residual.astype(jnp.bfloat16)
        for h in range(2):
            adjoint = jnp.dot(
                residual,
                back[:, h * piece : h * piece + piece],
                preferred_element_type=jnp.float32,
            )
            spec = cross[h, rows, :].astype(jnp.float32)
            out_ref[rows, h * bins : h * bins + bins] = (
                adjoint[:, :bins] * spec[:, :bins] + adjoint[:, bins:] * spec[:, bins:]
            ).astype(jnp.bfloat16)
        return carry

    tiles = pairs // tile
    forward(0)
    push_own(1)
    share(0)
    finish(0)
    for copy in loads:
        copy.wait()
    lax.fori_loop(0, tiles // 2, first_piece, 0)
    forward(1)
    lax.fori_loop(tiles // 2, tiles, first_piece, 0)
    whiten(1, me)
    share(1)
    finish(1)
    lax.fori_loop(0, tiles, second_piece, 0)
    for copy in sent:
        copy.wait_send()


def sum_kernel(
    stations, owner_ref, slot_ref, kernel_ref, out_ref,
    sums, side_send, side_recv, diag_send, diag_across, diag_along, far_send, far_recv,
    side_ss, side_rs, send_sem, recv_sem,
):
    me = lax.axis_index("pairs")
    across, along, diagonal, sibling = neighbours(me)
    groups = kernel_ref.shape[1] // 128
    half = stations // 2
    shift = 1 - 2 * (me % 2)

    barrier = pltpu.get_barrier_semaphore()
    for peer in (across, along, sibling):
        pl.semaphore_signal(barrier, inc=1, device_id={"pairs": peer}, device_id_type=MESH)
    pl.semaphore_wait(barrier, 3)

    def partial(owner):
        here = lax.broadcasted_iota(jnp.int32, (stations, slot_ref.shape[1]), 0)
        place = jnp.where(owner_ref[...] == owner, slot_ref[...], -1)
        hit = (here == place[0:1, :]) | (here == place[1:2, :])
        return jnp.dot(
            hit.astype(jnp.bfloat16), kernel_ref[...], preferred_element_type=jnp.float32
        )

    def send(src, dst, sem, target):
        copy = pltpu.make_async_remote_copy(
            src_ref=src, dst_ref=dst, send_sem=send_sem.at[sem], recv_sem=recv_sem.at[sem],
            device_id={"pairs": target}, device_id_type=MESH,
        )
        copy.start()
        return copy

    low, high = pl.ds(0, half), pl.ds(half, half)
    sides = []

    def chip_sum(q, chip):
        side_send[q] = partial(chip + shift).astype(jnp.bfloat16)
        copy = pltpu.make_async_remote_copy(
            src_ref=side_send.at[q], dst_ref=side_recv.at[q], send_sem=side_ss.at[q],
            recv_sem=side_rs.at[q], device_id={"pairs": sibling}, device_id_type=MESH,
        )
        copy.start()
        sides.append(copy)

        sums[q] = partial(chip)
        copy.wait_recv()

    def whole(q, rows):
        return sums[q, rows, :] + side_recv[q, rows, :].astype(jnp.float32)

    chip_sum(0, diagonal)
    diag_send[low, :] = whole(0, low).astype(jnp.bfloat16)
    to_across = send(diag_send.at[low], diag_across, 0, across)
    diag_send[high, :] = whole(0, high).astype(jnp.bfloat16)
    to_along = send(diag_send.at[high], diag_along, 1, along)

    chip_sum(1, across)
    far_send[0, low, :] = whole(1, low).astype(jnp.bfloat16)
    first_across = send(far_send.at[0, low], far_recv.at[0, low], 2, across)
    chip_sum(2, along)
    far_send[1, high, :] = whole(2, high).astype(jnp.bfloat16)
    first_along = send(far_send.at[1, high], far_recv.at[1, high], 3, along)

    to_along.wait_recv()
    far_send[0, high, :] = (whole(1, high) + diag_along[...].astype(jnp.float32)).astype(
        jnp.bfloat16
    )
    last_across = send(far_send.at[0, high], far_recv.at[0, high], 4, across)
    to_across.wait_recv()
    far_send[1, low, :] = (whole(2, low) + diag_across[...].astype(jnp.float32)).astype(
        jnp.bfloat16
    )
    last_along = send(far_send.at[1, low], far_recv.at[1, low], 5, along)

    chip_sum(3, me)
    for copy in (first_across, first_along, last_across, last_along):
        copy.wait_recv()
    for first in (0, half):
        rows = pl.ds(first, half)
        result = (
            whole(3, rows)
            + far_recv[0, rows, :].astype(jnp.float32)
            + far_recv[1, rows, :].astype(jnp.float32)
        )
        for j in range(groups):
            out_ref[pl.ds(first * groups + j, half, stride=groups), :] = result[
                :, j * 128 : j * 128 + 128
            ]
    for copy in (to_across, to_along, first_across, first_along, last_across, last_along):
        copy.wait_send()
    for copy in sides:
        copy.wait_send()


def quarter_kernel(sums_ref, out_ref):
    out_ref[...] = 0.25 * sums_ref[...]


def chip_shards(spectra, observed, pair_owner, pair_slot, win_start, win_end):
    owners = lax.axis_size("pairs")
    bands = lax.axis_size("band")
    stations, _, width = spectra.shape
    half = width // 2
    pairs, _, lags = observed.shape
    tile = min(512, pairs)
    bf16, f32 = jnp.bfloat16, jnp.float32
    vmem = pl.BlockSpec(memory_space=pltpu.VMEM)
    hbm = pl.BlockSpec(memory_space=pl.ANY)
    dma = pltpu.SemaphoreType.DMA

    table = basis_constant(half, lags).reshape(2, 2, half // 2, lags)
    table = table.transpose(1, 0, 2, 3).reshape(width, lags)
    owner_rows, slot_rows = pair_owner.T, pair_slot.T

    with jax.named_scope("pair_kernels"):
        kernels = pl.pallas_call(
            functools.partial(pair_kernel, bands, owners, tile),
            out_shape=jax.ShapeDtypeStruct((pairs, half), bf16),
            in_specs=[vmem, pl.BlockSpec(memory_space=pltpu.SMEM), vmem, vmem] + [hbm] * 3,
            out_specs=vmem,
            scratch_shapes=[
                pltpu.VMEM((2, owners, stations, half), bf16),
                pltpu.VMEM((owners * stations, width // 128, 128), f32),
                pltpu.VMEM((tile * width // 128, 128), f32),
                pltpu.VMEM((tile * width // 128, 128), f32),
                pltpu.VMEM((2, pairs, half), bf16),
                pltpu.VMEM((pairs, lags), f32),
                pltpu.VMEM((pairs, lags), bf16),
                pltpu.VMEM((width, lags), bf16),
                pltpu.VMEM((lags, width), bf16),
                pltpu.VMEM((pairs, 2), jnp.int32),
                pltpu.VMEM((8, stations), f32),
                pltpu.VMEM((bands, 8, stations), f32),
                pltpu.VMEM((8, stations), f32),
                pltpu.VMEM((owners, 8, stations), f32),
                dma((3,)), dma((20,)), dma((20,)), dma((bands,)), dma((bands,)),
                dma((owners,)), dma((owners,)),
            ],
            compiler_params=pltpu.CompilerParams(
                collective_id=0, has_side_effects=True, vmem_limit_bytes=VMEM_LIMIT
            ),
        )(
            spectra.reshape(stations, width),
            owner_rows * stations + slot_rows,
            win_start.reshape(1, pairs),
            win_end.reshape(1, pairs),
            observed.reshape(pairs, lags),
            jnp.asarray(table, bf16),
            jnp.asarray(table.T, bf16),
        )

    with jax.named_scope("station_sums"):
        out = pl.pallas_call(
            functools.partial(sum_kernel, stations),
            out_shape=jax.ShapeDtypeStruct((stations * half // 128, 128), f32),
            in_specs=[vmem] * 3,
            out_specs=vmem,
            scratch_shapes=[
                pltpu.VMEM((4, stations, half), f32),
                pltpu.VMEM((4, stations, half), bf16),
                pltpu.VMEM((4, stations, half), bf16),
                pltpu.VMEM((stations, half), bf16),
                pltpu.VMEM((stations // 2, half), bf16),
                pltpu.VMEM((stations // 2, half), bf16),
                pltpu.VMEM((2, stations, half), bf16),
                pltpu.VMEM((2, stations, half), bf16),
                dma((4,)), dma((4,)), dma((6,)), dma((6,)),
            ],
            compiler_params=pltpu.CompilerParams(
                collective_id=1, has_side_effects=True, vmem_limit_bytes=VMEM_LIMIT
            ),
        )(owner_rows, slot_rows, kernels)
    block = pl.BlockSpec((out.shape[0] // 2, 128), lambda i: (i, 0))
    with jax.named_scope("quarter"):
        out = pl.pallas_call(
            quarter_kernel,
            out_shape=jax.ShapeDtypeStruct(out.shape, f32),
            grid=(2,),
            in_specs=[block],
            out_specs=block,
        )(out)
    return out.reshape(stations, 1, half)


def lag_basis(half_width, lag_count):
    freqs = jnp.arange(half_width, dtype=jnp.int32)
    lag_index = jnp.arange(lag_count, dtype=jnp.int32)
    phases = (freqs[:, None] * lag_index[None, :] % lag_count).astype(jnp.float32) * (
        2.0 * math.pi / lag_count
    )
    factor = 1.0 / math.sqrt(lag_count)
    return jnp.concatenate([jnp.cos(phases) * factor, -jnp.sin(phases) * factor], axis=0).astype(
        jnp.bfloat16
    )


def owner_positions(owner_flat, owner_count):
    onehot = (owner_flat[:, None] == jnp.arange(owner_count, dtype=jnp.int32)[None, :]).astype(
        jnp.int32
    )
    before = jnp.cumsum(onehot, axis=0) - onehot
    return jnp.sum(before * onehot, axis=1)


def shards(spectra, observed, pair_owner, pair_slot, win_start, win_end):
    owners = lax.axis_size("pairs")
    station_count = spectra.shape[0]
    band_count = spectra.shape[1]
    full_width = spectra.shape[2]
    half_width = full_width // 2
    pair_count = observed.shape[0]
    lag_count = observed.shape[2]
    capacity = 3 * pair_count // owners
    spectrum = spectra.astype(jnp.float32)
    local_power = jnp.sum(spectrum * spectrum, axis=(1, 2))
    total_power = lax.psum(local_power, "band")
    entries = band_count * lax.axis_size("band") * full_width
    whitened = (spectrum * lax.rsqrt(total_power / entries + 1e-05)[:, None, None]).astype(
        jnp.bfloat16
    )
    owner_flat = pair_owner.reshape(-1)
    slot_flat = pair_slot.reshape(-1)
    position = owner_positions(owner_flat, owners)
    request = (
        jnp.full((owners, capacity), station_count, jnp.int32)
        .at[owner_flat, position]
        .set(slot_flat)
    )
    wanted = lax.all_to_all(request, "pairs", split_axis=0, concat_axis=0, tiled=True)
    panel_rows = lax.all_gather(whitened, "pairs", axis=0, tiled=True)
    fetched = panel_rows[owner_flat * station_count + slot_flat]
    fetched = fetched.reshape(pair_count, 2, band_count, full_width)
    near_end = fetched[:, 0].astype(jnp.float32)
    far_end = fetched[:, 1].astype(jnp.float32)
    near_re, near_im = (near_end[..., :half_width], near_end[..., half_width:])
    far_re, far_im = (far_end[..., :half_width], far_end[..., half_width:])
    cross_spec = jnp.concatenate(
        [near_re * far_re + near_im * far_im, near_im * far_re - near_re * far_im], axis=-1
    ).astype(jnp.bfloat16)
    table = lag_basis(half_width, lag_count)
    lagged = jnp.einsum("pbf,ft->pbt", cross_spec, table, preferred_element_type=jnp.float32)
    lag_index = jnp.arange(lag_count, dtype=jnp.int32)
    window = (
        (lag_index[None, :] >= win_start[:, None]) & (lag_index[None, :] < win_end[:, None])
    ).astype(jnp.float32)
    residual = (window[:, None, :] * (lagged - observed.astype(jnp.float32))).astype(jnp.bfloat16)
    adjoint = jnp.einsum("pbt,ft->pbf", residual, table, preferred_element_type=jnp.float32)
    adj_re, adj_im = (adjoint[..., :half_width], adjoint[..., half_width:])
    to_first = jnp.concatenate(
        [adj_re * far_re - adj_im * far_im, adj_re * far_im + adj_im * far_re], axis=-1
    ).astype(jnp.bfloat16)
    to_second = jnp.concatenate(
        [adj_re * near_re + adj_im * near_im, adj_re * near_im - adj_im * near_re], axis=-1
    ).astype(jnp.bfloat16)
    stacked = jnp.stack([to_first, to_second], axis=1).reshape(
        2 * pair_count, band_count, full_width
    )
    outgoing = (
        jnp.zeros((owners, capacity, band_count, full_width), jnp.bfloat16)
        .at[owner_flat, position]
        .set(stacked)
    )
    incoming = lax.all_to_all(outgoing, "pairs", split_axis=0, concat_axis=0, tiled=True)

    def add_source(source, summed):
        block_rows = lax.dynamic_index_in_dim(incoming, source, 0, keepdims=False).astype(
            jnp.float32
        )
        block_ids = lax.dynamic_index_in_dim(wanted, source, 0, keepdims=False)
        return summed.at[block_ids].add(block_rows)

    summed = lax.fori_loop(
        0, owners, add_source, jnp.zeros((station_count + 1, band_count, full_width), jnp.float32)
    )
    summed = summed[:station_count]
    own_spec = whitened.astype(jnp.float32)
    return 0.25 * (
        summed[..., :half_width] * own_spec[..., :half_width]
        + summed[..., half_width:] * own_spec[..., half_width:]
    )


def solution(mesh):
    square_of_chips = mesh.shape["pairs"] == 8
    return jax.shard_map(
        chip_shards if square_of_chips else shards,
        mesh=mesh,
        in_specs=(
            P("pairs", "band", None),
            P("pairs", "band", None),
            P("pairs", None),
            P("pairs", None),
            P("pairs"),
            P("pairs"),
        ),
        out_specs=P("pairs", "band", None),
        check_vma=False,
    )
```
